32 devices in a mesh: dp: 4 (over x, core), ex: 2 (over y), ey: 4 (over z).
Axes of the slice: x: 2, y: 2, z: 4, core: 2. Of those that a mesh axis runs over, the one named last changes fastest.
Arguments:
- tokens: bfloat16 [2, 1536, 2048], P(None, ('dp', 'ex', 'ey')), parts along dimension 1, may hold values from -6 to 6
- expert_ids: int32 [2, 1536, 8], P(None, ('dp', 'ex', 'ey')), parts along dimension 1, may hold values from 0 to 7, as said below
- slot_ids: int32 [2, 1536, 8], P(None, ('dp', 'ex', 'ey')), parts along dimension 1, may hold values from 0 to 47, as said below
- gate_values: float32 [2, 1536, 8], P(None, ('dp', 'ex', 'ey')), parts along dimension 1, may hold values from 0.05 to 1
- gate_weight: bfloat16 [8, 2048, 1024], P(('ex', 'ey')), may hold values from -0.125 to 0.125
- up_weight: bfloat16 [8, 2048, 1024], P(('ex', 'ey')), may hold values from -0.125 to 0.125
- down_weight: bfloat16 [8, 1024, 2048], P(('ex', 'ey')), may hold values from -0.1875 to 0.1875
Outputs:
- mixture: bfloat16 [2, 1536, 2048], P(None, ('dp', 'ex', 'ey')), parts along dimension 1
The draws below stay inside these ranges and needn't reach their ends.
There are 4 independent parts, one for each index of `dp`. The reference program is written for one: setup_inputs(seed, part) draws one part's arguments, and reference() takes and returns one part's arrays. A program takes and returns all parts, laid end to end along the dimension named above; an argument that names none is the same for every part. Nothing has to cross between parts.
Inputs may be any that keep to these rules, and one draw needn't show every extreme that they name: `expert_ids`: each token names 8 different experts. `slot_ids`: within one micro-batch, one block of 48 tokens and one expert, the assignments are numbered 0, 1, 2, ... in a drawn priority order; an assignment keeps its number as slot if it is below 60, else it is -1. In every block some expert receives an assignment from each of its 48 tokens.
All inputs are finite; a program needn't handle non-finite values.
Results may differ from the reference program's by a relative error of at most 0.0057.
Values may be sent and summed in bfloat16 or wider, within the bound.
No kernel may reach another device: no remote copies, remote signals or barrier semaphores. Data moves between devices by JAX's collectives and lax.ppermute only.
A program may use at most 64 MiB of HBM per device.

```python
import jax
import jax.numpy as jnp
from jax import lax

D = 2048
HID = 1024
TOP = 8
MICRO = 2
TOK_DEV = 48
EXPERTS = 8
TOKENS = 384
SLOTS = 60


def routing_draw(key):
    key_bias, key_noise, key_hot, key_order = jax.random.split(key, 4)
    hot_expert = jax.random.randint(key_hot, (), 0, EXPERTS)
    expert_bias = jax.random.randint(key_bias, (EXPERTS,), 0, 1 << 14)
    token_noise = jax.random.randint(key_noise, (MICRO, TOKENS, EXPERTS), 0, 1 << 14)
    column = jnp.arange(EXPERTS, dtype=jnp.int32)
    scores = (token_noise + expert_bias[None, None, :] + jnp.where(column == hot_expert, 1 << 16, 0)[None, None, :]) * EXPERTS + column[None, None, :]
    chosen = lax.top_k(scores, TOP)[1].astype(jnp.int32)
    length = TOK_DEV * TOP
    blocks = TOKENS // TOK_DEV
    flat_chosen = chosen.reshape(MICRO, blocks, length)
    position = jnp.arange(length, dtype=jnp.int32)
    priority = jax.random.randint(key_order, (MICRO, blocks, length), 0, 1 << 12) * length + position[None, None, :]
    same = flat_chosen[..., :, None] == flat_chosen[..., None, :]
    before = priority[..., None, :] < priority[..., :, None]
    number = jnp.sum((same & before).astype(jnp.int32), axis=-1).reshape(MICRO, TOKENS, TOP)
    places = jnp.where(number < SLOTS, number, -1).astype(jnp.int32)
    return (chosen, places)


def draw_expert_ids(key, part):
    return routing_draw(key)[0]


def draw_slot_ids(key, part):
    return routing_draw(key)[1]


def shard_levels(key, dims, pieces, low, high):
    gain = 1.0
    for dim, parts in pieces:
        heights = jax.random.uniform(jax.random.fold_in(jax.random.fold_in(key, 6), dim), (parts,), jnp.float32, low / len(pieces), high / len(pieces))
        gain = gain * jnp.repeat(jnp.exp(heights), dims[dim] // parts).reshape((-1,) + (1,) * (len(dims) - 1 - dim))
    return gain


def centred(stream_key, dims, deviation, reach, shards=(), held_as=jnp.bfloat16):
    gain = shard_levels(stream_key, dims, shards, -0.22, 0.18) if shards else 1.0
    result = jax.random.normal(stream_key, dims, jnp.float32) * deviation * gain
    return jnp.minimum(jnp.maximum(result, -reach), reach).astype(held_as)


def setup_inputs(seed: int = 0, part: int = 0) -> dict:
    splits = jax.random.split(jax.random.key(seed), 8)
    part_splits = jax.random.split(jax.random.fold_in(splits[7], part), 8)
    tokens = centred(part_splits[0], (MICRO, TOKENS, D), 1.0, 6.0, ((1, 8),))
    expert_ids = draw_expert_ids(jax.random.fold_in(jax.random.fold_in(splits[7], part), 71), part)
    slot_ids = draw_slot_ids(jax.random.fold_in(jax.random.fold_in(splits[7], part), 71), part)
    gate_values = jnp.clip(0.05 + 0.95 * jax.random.uniform(part_splits[3], (MICRO, TOKENS, TOP), jnp.float32) ** shard_levels(part_splits[3], (MICRO, TOKENS, TOP), ((1, 8),), -0.2, 0.2), 0.05, 1.0)
    gate_weight = centred(splits[4], (EXPERTS, D, HID), D ** -0.5, 0.125, ((0, 8),))
    up_weight = centred(splits[5], (EXPERTS, D, HID), D ** -0.5, 0.125, ((0, 8),))
    down_weight = centred(splits[6], (EXPERTS, HID, D), HID ** -0.5, 0.1875, ((0, 8),))
    return {"tokens": tokens, "expert_ids": expert_ids, "slot_ids": slot_ids, "gate_values": gate_values, "gate_weight": gate_weight, "up_weight": up_weight, "down_weight": down_weight}


def expert_block(packed):
    rows, gate_matrix, up_matrix, down_matrix = packed
    flat = rows.reshape(-1, D)
    gate_part = jnp.dot(flat, gate_matrix, preferred_element_type=jnp.float32)
    up_part = jnp.dot(flat, up_matrix, preferred_element_type=jnp.float32)
    hidden = (jax.nn.silu(gate_part) * up_part).astype(jnp.bfloat16)
    output = jnp.dot(hidden, down_matrix, preferred_element_type=jnp.float32).astype(jnp.bfloat16)
    return output.reshape(rows.shape)


def reference(tokens, expert_ids, slot_ids, gate_values, gate_weight, up_weight, down_weight):
    sources = TOKENS // TOK_DEV
    source = jnp.broadcast_to((jnp.arange(TOKENS, dtype=jnp.int32) // TOK_DEV)[:, None], (TOKENS, TOP))
    results = []
    for index in range(MICRO):
        chosen = expert_ids[index]
        places = slot_ids[index]
        kept_mask = places >= 0
        slot_place = jnp.where(kept_mask, places, SLOTS).astype(jnp.int32)
        copies = jnp.broadcast_to(tokens[index][:, None, :], (TOKENS, TOP, D))
        buffer = jnp.zeros((EXPERTS, sources, SLOTS, D), jnp.bfloat16)
        buffer = buffer.at[chosen, source, slot_place].set(copies, mode="drop")
        answers = lax.map(expert_block, (buffer, gate_weight, up_weight, down_weight))
        picked = answers[chosen, source, jnp.where(kept_mask, places, 0).astype(jnp.int32)]
        weighting = jnp.where(kept_mask, gate_values[index], jnp.float32(0.0)).astype(jnp.float32)
        mixture = jnp.einsum("tk,tkd->td", weighting, picked.astype(jnp.float32), precision=lax.Precision.HIGHEST)
        results.append(mixture.astype(jnp.bfloat16))
    return jnp.stack(results, axis=0)
```

```python
import functools

import jax
import jax.numpy as jnp
from jax import lax
from jax.experimental import pallas as pl
from jax.experimental.pallas import tpu as pltpu
from jax.sharding import PartitionSpec as P

TOP = 8


def slot_layer(tokens, expert_ids, slot_ids, gate_values, gate_weight, up_weight, down_weight):
    across_x = lax.axis_size("ex")
    across_y = lax.axis_size("ey")
    experts = across_x * across_y
    micro, tok_dev, width = tokens.shape
    slot_count = (tok_dev * TOP * 5 + 4 * experts - 1) // (4 * experts)
    cells = experts * slot_count
    gate_matrix = gate_weight[0]
    up_matrix = up_weight[0]
    down_matrix = down_weight[0]
    columns = jnp.arange(cells, dtype=jnp.int32)

    def expert_apply(received):
        flat = received.reshape(-1, width)
        gate_part = jnp.dot(flat, gate_matrix, preferred_element_type=jnp.float32)
        up_part = jnp.dot(flat, up_matrix, preferred_element_type=jnp.float32)
        hidden = (jax.nn.silu(gate_part) * up_part).astype(jnp.bfloat16)
        output = jnp.dot(hidden, down_matrix, preferred_element_type=jnp.float32).astype(
            jnp.bfloat16
        )
        return output.reshape(received.shape)

    def route_slots(buffer):
        return lax.all_to_all(
            expert_apply(
                lax.all_to_all(buffer, ("ex", "ey"), split_axis=0, concat_axis=0, tiled=True)
            ),
            ("ex", "ey"),
            split_axis=0,
            concat_axis=0,
            tiled=True,
        )

    buffers = []
    mixings = []
    for index in range(micro):
        chosen = expert_ids[index]
        places = slot_ids[index]
        cell_index = jnp.where(places >= 0, chosen * slot_count + places, -1)
        one_hot = cell_index[:, :, None] == columns[None, None, :]
        selection = jnp.sum(one_hot.astype(jnp.float32), axis=1).astype(jnp.bfloat16)
        mixing = jnp.sum(
            jnp.where(one_hot, gate_values[index][:, :, None], jnp.float32(0.0)), axis=1
        )
        gathered = jnp.dot(selection.T, tokens[index], preferred_element_type=jnp.float32)
        buffers.append(gathered.astype(jnp.bfloat16).reshape(experts, slot_count, width))
        mixings.append(mixing)
    outputs = [route_slots(buffers[index]) for index in range(micro)]
    results = []
    for index in range(micro):
        flat_out = outputs[index].reshape(cells, width).astype(jnp.float32)
        mixture = jnp.dot(mixings[index], flat_out, precision=lax.Precision.HIGHEST)
        results.append(mixture.astype(jnp.bfloat16))
    return jnp.stack(results, axis=0)


def pack_kernel(tokens_ref, *refs):
    micro, tok_dev, width = tokens_ref.shape
    routing = refs[:3]
    blocks = refs[3 : 3 + micro]
    ids_ref, slots_ref, gates_ref, spread_ref, small_semaphores, semaphores = refs[3 + micro :]
    choices = ids_ref.shape[1]
    small_copies = [
        pltpu.make_async_copy(source, target, small_semaphores.at[index])
        for index, (source, target) in enumerate(zip(routing, (ids_ref, slots_ref, gates_ref)))
    ]
    rows = blocks[0].shape[0]
    groups = tok_dev // rows
    copies = [
        pltpu.make_async_copy(
            tokens_ref.at[index, pl.ds(group * rows, rows)],
            block.at[:, pl.ds(group * width, width)],
            semaphores.at[index, group],
        )
        for index, block in enumerate(blocks)
        for group in range(groups)
    ]
    for copy in small_copies + copies:
        copy.start()
    for copy in small_copies:
        copy.wait()
    names = lax.broadcasted_iota(jnp.int32, (choices, tok_dev), 0)
    for index, block in enumerate(blocks):
        ids = ids_ref[index]
        kept = jnp.where(slots_ref[index] >= 0, gates_ref[index], jnp.float32(0.0))
        share = jnp.zeros((choices, tok_dev), jnp.float32)
        for choice in range(choices):
            share += jnp.where(
                ids[choice : choice + 1] == names, kept[choice : choice + 1], jnp.float32(0.0)
            )
        spread_ref[...] = jnp.zeros_like(spread_ref)
        for piece in range(3):
            rounded = share.astype(jnp.bfloat16).astype(jnp.float32)
            share = share - rounded
            for group in range(groups):
                place = (group * 3 + piece) * choices
                spread_ref[pl.ds(place, choices), pl.ds(0, rows)] = rounded[
                    :, group * rows : (group + 1) * rows
                ]
        block[:, pl.ds(groups * width, 128)] = spread_ref[...].T[:rows].astype(jnp.bfloat16)
    for copy in copies:
        copy.wait()


def pack(tokens, expert_ids, slot_ids, gate_values):
    micro, tok_dev, width = tokens.shape
    rows = 16
    groups = tok_dev // rows
    columns = [
        jnp.transpose(array, (0, 2, 1)) for array in (expert_ids, slot_ids, gate_values)
    ]
    outside = [
        pltpu.with_memory_space_constraint(array, pltpu.HBM) for array in [tokens] + columns
    ]
    inside = pl.BlockSpec(memory_space=pltpu.VMEM)
    return pl.pallas_call(
        pack_kernel,
        in_specs=[pl.BlockSpec(memory_space=pl.ANY)] * len(outside),
        out_specs=[inside] * micro,
        out_shape=[pltpu.VMEM((rows, groups * width + 128), jnp.bfloat16)] * micro,
        scratch_shapes=[pltpu.VMEM(array.shape, array.dtype) for array in columns]
        + [
            pltpu.VMEM((128, 128), jnp.float32),
            pltpu.SemaphoreType.DMA((len(columns),)),
            pltpu.SemaphoreType.DMA((micro, groups)),
        ],
        compiler_params=pltpu.CompilerParams(vmem_limit_bytes=4 * 1024 * 1024),
        cost_estimate=pl.CostEstimate(
            flops=10000000000, bytes_accessed=0, transcendentals=0
        ),
    )(*outside)


def pass_on(block, stride):
    across_x = lax.axis_size("ex")
    across_y = lax.axis_size("ey")
    ring = []
    for row in range(across_x):
        places = [row * across_y + column for column in range(across_y)]
        ring += places if row % 2 == 0 else places[::-1]
    count = len(ring)
    pairs = [(ring[index], ring[(index + stride) % count]) for index in range(count)]
    return lax.ppermute(block, ("ex", "ey"), pairs)


def mark_kernel(marker_ref):
    marker_ref[...] = jnp.zeros_like(marker_ref)


def mark():
    return pl.pallas_call(
        mark_kernel,
        out_specs=pl.BlockSpec(memory_space=pltpu.VMEM),
        out_shape=pltpu.VMEM((8, 128), jnp.float32),
        compiler_params=pltpu.CompilerParams(vmem_limit_bytes=1024 * 1024),
        cost_estimate=pl.CostEstimate(flops=0, bytes_accessed=25000000, transcendentals=0),
    )()


def expert_kernel(count, *refs):
    blocks = refs[:count]
    gate_ref, up_ref, down_ref = refs[count : count + 3]
    rows_ref, weight_ref, hidden_ref = refs[-3:]
    outputs = refs[-3 - count : -3]
    _, width, hidden_width = gate_ref.shape
    rows = blocks[0].shape[0]
    groups = blocks[0].shape[1] // width
    tok_dev = rows * groups
    part = 256

    me = lax.axis_index("ex") * lax.axis_size("ey") + lax.axis_index("ey")
    experts = lax.axis_size("ex") * lax.axis_size("ey")
    lane = lax.broadcasted_iota(jnp.int32, (rows, 128), 1)
    for index, block in enumerate(blocks):
        gates = block[:, groups * width :].astype(jnp.float32)
        for group in range(groups):
            span = pl.ds(index * tok_dev + group * rows, rows)
            rows_ref[span, :] = block[:, group * width : (group + 1) * width]
            mine = lane < 0
            for piece in range(3):
                mine = mine | (lane == me + (group * 3 + piece) * experts)
            weight_ref[span, :] = jnp.broadcast_to(
                jnp.sum(jnp.where(mine, gates, jnp.float32(0.0)), axis=-1, keepdims=True),
                (rows, 128),
            )

    for start in range(0, hidden_width, part):
        columns = pl.ds(start, part)
        tokens = rows_ref[...]
        gate_part = jnp.dot(tokens, gate_ref[0, :, columns], preferred_element_type=jnp.float32)
        up_part = jnp.dot(tokens, up_ref[0, :, columns], preferred_element_type=jnp.float32)
        hidden_ref[:, columns] = (jax.nn.silu(gate_part) * up_part).astype(jnp.bfloat16)

    for start in range(0, width, part):
        columns = pl.ds(start, part)
        output = jnp.dot(
            hidden_ref[...], down_ref[0, :, columns], preferred_element_type=jnp.float32
        )
        output = output * weight_ref[:, :1]
        for index, out in enumerate(outputs):
            out[:, columns] = output[index * tok_dev : (index + 1) * tok_dev].astype(out.dtype)


def run_expert(blocks, kinds, earlier, weights):
    count = len(blocks)
    _, width, hidden = weights[0].shape
    tok_dev = blocks[0].shape[0] * (blocks[0].shape[1] // width)
    rows = count * tok_dev
    inside = [pltpu.with_memory_space_constraint(array, pltpu.VMEM) for array in blocks + weights]
    in_vmem = pl.BlockSpec(memory_space=pltpu.VMEM)
    out_shape = [pltpu.VMEM((tok_dev, width), kind) for kind in kinds]
    return pl.pallas_call(
        functools.partial(expert_kernel, count),
        in_specs=[in_vmem] * len(inside) + [pl.BlockSpec(memory_space=pl.ANY)] * len(earlier),
        out_specs=[in_vmem] * len(out_shape),
        out_shape=out_shape,
        scratch_shapes=[
            pltpu.VMEM((rows, width), jnp.bfloat16),
            pltpu.VMEM((rows, 128), jnp.float32),
            pltpu.VMEM((rows, hidden), jnp.bfloat16),
        ],
        compiler_params=pltpu.CompilerParams(vmem_limit_bytes=16 * 1024 * 1024),
        cost_estimate=pl.CostEstimate(
            flops=6 * rows * width * hidden,
            bytes_accessed=6 * width * hidden + 6 * rows * width,
            transcendentals=rows * hidden,
        ),
    )(*inside, *earlier)


def after(array, others):
    return lax.optimization_barrier([array] + list(others))[0]


def dense_layer(tokens, expert_ids, slot_ids, gate_values, gate_weight, up_weight, down_weight):
    experts = lax.axis_size("ex") * lax.axis_size("ey")
    micro = tokens.shape[0]

    packed = pack(tokens, expert_ids, slot_ids, gate_values)

    long_chains = [(index, 1 if index % 2 == 0 else -1) for index in range(micro)]
    short_chains = [(index, -stride) for index, stride in long_chains]
    chains = long_chains + short_chains[::-1]
    long_reach, short_reach = experts // 2, (experts - 1) // 2

    gathered = [{0: packed[index]} for index in range(micro)]
    outputs = [{} for index in range(micro)]
    carried = {}

    def gather_hop(some, hop, others):
        for index, stride in some:
            block = gathered[index][-(hop - 1) * stride]
            with jax.named_scope(f"gather{index}_{stride:+d}_hop{hop}"):
                gathered[index][-hop * stride] = pass_on(after(block, others), stride)
            others = others

    def sum_hop(some, left, others):
        sent = []
        for index, stride in some:
            partial = outputs[index][-left * stride]
            before = []
            if (index, stride) in carried:
                before = [carried[index, stride]]
                partial = partial + carried[index, stride].astype(jnp.float32)
            partial = after(partial.astype(jnp.bfloat16), others)
            with jax.named_scope(f"sum{index}_{-stride:+d}_left{left}"):
                carried[index, stride] = pass_on(partial, -stride)
            sent.append(partial)
            others = others
        return sent

    def expert(some, hops, earlier):
        keys = [(index, -hop * stride) for hop in hops for index, stride in some]
        keys = list(dict.fromkeys(keys))
        first = {(index, -long_reach * stride) for index, stride in long_chains}
        first |= {(index, -short_reach * stride) for index, stride in short_chains}
        answers = run_expert(
            [gathered[index][place] for index, place in keys],
            [jnp.bfloat16 if key in first else jnp.float32 for key in keys],
            earlier,
            weights,
        )
        for (index, place), answer in zip(keys, answers):
            outputs[index][place] = answer
        return [answers[0]]

    weights = [gate_weight, up_weight, down_weight]
    marker = mark()
    done = []
    for hop in range(1, short_reach + 1):
        gather_hop(long_chains, hop, [marker])
        gather_hop(short_chains[::-1], hop, [])
        if hop == short_reach - 1:
            done = expert(chains, range(short_reach - 2, -1, -1), [])
    done = expert(chains, [short_reach - 1], done)
    gather_hop(long_chains, long_reach, done)
    done = expert(long_chains, [short_reach], done)
    done = expert(short_chains[::-1], [short_reach], done)
    last = [gathered[index][-long_reach * stride] for index, stride in long_chains]
    done = expert(long_chains, [long_reach], done)
    for left in range(long_reach, 0, -1):
        sent = sum_hop(long_chains, left, [])
        if left > 1:
            sent = sum_hop(short_chains[:1], left - 1, last + sent)
            sum_hop(short_chains[1:], left - 1, last + sent)

    results = []
    for index in range(micro):
        total = outputs[index][0]
        for stride in (1, -1):
            total = total + carried[index, stride].astype(jnp.float32)
        results.append(total.astype(jnp.bfloat16))
    return jnp.stack(results, axis=0)


def per_device(tokens, expert_ids, slot_ids, gate_values, gate_weight, up_weight, down_weight):
    experts = lax.axis_size("ex") * lax.axis_size("ey")
    layer = dense_layer if experts == expert_ids.shape[-1] else slot_layer
    return layer(
        tokens, expert_ids, slot_ids, gate_values, gate_weight, up_weight, down_weight
    )


def solution(mesh):
    in_specs = (
        P(None, ("dp", "ex", "ey"), None),
        P(None, ("dp", "ex", "ey"), None),
        P(None, ("dp", "ex", "ey"), None),
        P(None, ("dp", "ex", "ey"), None),
        P(("ex", "ey"), None, None),
        P(("ex", "ey"), None, None),
        P(("ex", "ey"), None, None),
    )
    out_specs = P(None, ("dp", "ex", "ey"), None)
    return jax.shard_map(
        per_device, mesh=mesh, in_specs=in_specs, out_specs=out_specs, check_vma=False
    )
```

```python
import functools

import jax
import jax.numpy as jnp
from jax import lax
from jax.experimental import pallas as pl
from jax.experimental.pallas import tpu as pltpu
from jax.sharding import PartitionSpec as P

TOP = 8


def slot_layer(tokens, expert_ids, slot_ids, gate_values, gate_weight, up_weight, down_weight):
    across_x = lax.axis_size("ex")
    across_y = lax.axis_size("ey")
    experts = across_x * across_y
    micro, tok_dev, width = tokens.shape
    slot_count = (tok_dev * TOP * 5 + 4 * experts - 1) // (4 * experts)
    cells = experts * slot_count
    gate_matrix = gate_weight[0]
    up_matrix = up_weight[0]
    down_matrix = down_weight[0]
    columns = jnp.arange(cells, dtype=jnp.int32)

    def expert_apply(received):
        flat = received.reshape(-1, width)
        gate_part = jnp.dot(flat, gate_matrix, preferred_element_type=jnp.float32)
        up_part = jnp.dot(flat, up_matrix, preferred_element_type=jnp.float32)
        hidden = (jax.nn.silu(gate_part) * up_part).astype(jnp.bfloat16)
        output = jnp.dot(hidden, down_matrix, preferred_element_type=jnp.float32).astype(
            jnp.bfloat16
        )
        return output.reshape(received.shape)

    def route_slots(buffer):
        return lax.all_to_all(
            expert_apply(
                lax.all_to_all(buffer, ("ex", "ey"), split_axis=0, concat_axis=0, tiled=True)
            ),
            ("ex", "ey"),
            split_axis=0,
            concat_axis=0,
            tiled=True,
        )

    buffers = []
    mixings = []
    for index in range(micro):
        chosen = expert_ids[index]
        places = slot_ids[index]
        cell_index = jnp.where(places >= 0, chosen * slot_count + places, -1)
        one_hot = cell_index[:, :, None] == columns[None, None, :]
        selection = jnp.sum(one_hot.astype(jnp.float32), axis=1).astype(jnp.bfloat16)
        mixing = jnp.sum(
            jnp.where(one_hot, gate_values[index][:, :, None], jnp.float32(0.0)), axis=1
        )
        gathered = jnp.dot(selection.T, tokens[index], preferred_element_type=jnp.float32)
        buffers.append(gathered.astype(jnp.bfloat16).reshape(experts, slot_count, width))
        mixings.append(mixing)
    outputs = [route_slots(buffers[index]) for index in range(micro)]
    results = []
    for index in range(micro):
        flat_out = outputs[index].reshape(cells, width).astype(jnp.float32)
        mixture = jnp.dot(mixings[index], flat_out, precision=lax.Precision.HIGHEST)
        results.append(mixture.astype(jnp.bfloat16))
    return jnp.stack(results, axis=0)


def pack_kernel(tokens_ref, *refs):
    micro, tok_dev, width = tokens_ref.shape
    routing = refs[:3]
    blocks = refs[3 : 3 + micro]
    ids_ref, slots_ref, gates_ref, spread_ref, small_semaphores, semaphores = refs[3 + micro :]
    choices = ids_ref.shape[1]
    small_copies = [
        pltpu.make_async_copy(source, target, small_semaphores.at[index])
        for index, (source, target) in enumerate(zip(routing, (ids_ref, slots_ref, gates_ref)))
    ]
    rows = blocks[0].shape[0]
    groups = tok_dev // rows
    copies = [
        pltpu.make_async_copy(
            tokens_ref.at[index, pl.ds(group * rows, rows)],
            block.at[:, pl.ds(group * width, width)],
            semaphores.at[index, group],
        )
        for index, block in enumerate(blocks)
        for group in range(groups)
    ]
    for copy in small_copies + copies:
        copy.start()
    for copy in small_copies:
        copy.wait()
    names = lax.broadcasted_iota(jnp.int32, (choices, tok_dev), 0)
    for index, block in enumerate(blocks):
        ids = ids_ref[index]
        kept = jnp.where(slots_ref[index] >= 0, gates_ref[index], jnp.float32(0.0))
        share = jnp.zeros((choices, tok_dev), jnp.float32)
        for choice in range(choices):
            share += jnp.where(
                ids[choice : choice + 1] == names, kept[choice : choice + 1], jnp.float32(0.0)
            )
        spread_ref[...] = jnp.zeros_like(spread_ref)
        for piece in range(3):
            rounded = share.astype(jnp.bfloat16).astype(jnp.float32)
            share = share - rounded
            for group in range(groups):
                place = (group * 3 + piece) * choices
                spread_ref[pl.ds(place, choices), pl.ds(0, rows)] = rounded[
                    :, group * rows : (group + 1) * rows
                ]
        block[:, pl.ds(groups * width, 128)] = spread_ref[...].T[:rows].astype(jnp.bfloat16)
    for copy in copies:
        copy.wait()


def pack(tokens, expert_ids, slot_ids, gate_values):
    micro, tok_dev, width = tokens.shape
    rows = 16
    groups = tok_dev // rows
    columns = [
        jnp.transpose(array, (0, 2, 1)) for array in (expert_ids, slot_ids, gate_values)
    ]
    outside = [
        pltpu.with_memory_space_constraint(array, pltpu.HBM) for array in [tokens] + columns
    ]
    inside = pl.BlockSpec(memory_space=pltpu.VMEM)
    return pl.pallas_call(
        pack_kernel,
        in_specs=[pl.BlockSpec(memory_space=pl.ANY)] * len(outside),
        out_specs=[inside] * micro,
        out_shape=[pltpu.VMEM((rows, groups * width + 128), jnp.bfloat16)] * micro,
        scratch_shapes=[pltpu.VMEM(array.shape, array.dtype) for array in columns]
        + [
            pltpu.VMEM((128, 128), jnp.float32),
            pltpu.SemaphoreType.DMA((len(columns),)),
            pltpu.SemaphoreType.DMA((micro, groups)),
        ],
        compiler_params=pltpu.CompilerParams(vmem_limit_bytes=4 * 1024 * 1024),
        cost_estimate=pl.CostEstimate(
            flops=10000000000, bytes_accessed=0, transcendentals=0
        ),
    )(*outside)


def pass_on(block, stride):
    across_x = lax.axis_size("ex")
    across_y = lax.axis_size("ey")
    ring = []
    for row in range(across_x):
        places = [row * across_y + column for column in range(across_y)]
        ring += places if row % 2 == 0 else places[::-1]
    count = len(ring)
    pairs = [(ring[index], ring[(index + stride) % count]) for index in range(count)]
    return lax.ppermute(block, ("ex", "ey"), pairs)


def mark_kernel(marker_ref):
    marker_ref[...] = jnp.zeros_like(marker_ref)


def mark():
    return pl.pallas_call(
        mark_kernel,
        out_specs=pl.BlockSpec(memory_space=pltpu.VMEM),
        out_shape=pltpu.VMEM((8, 128), jnp.float32),
        compiler_params=pltpu.CompilerParams(vmem_limit_bytes=1024 * 1024),
        cost_estimate=pl.CostEstimate(flops=0, bytes_accessed=25000000, transcendentals=0),
    )()


def expert_kernel(count, *refs):
    blocks = refs[:count]
    gate_ref, up_ref, down_ref = refs[count : count + 3]
    rows_ref, weight_ref, hidden_ref = refs[-3:]
    outputs = refs[-3 - count : -3]
    _, width, hidden_width = gate_ref.shape
    rows = blocks[0].shape[0]
    groups = blocks[0].shape[1] // width
    tok_dev = rows * groups
    part = 256

    me = lax.axis_index("ex") * lax.axis_size("ey") + lax.axis_index("ey")
    experts = lax.axis_size("ex") * lax.axis_size("ey")
    lane = lax.broadcasted_iota(jnp.int32, (rows, 128), 1)
    for index, block in enumerate(blocks):
        gates = block[:, groups * width :].astype(jnp.float32)
        for group in range(groups):
            span = pl.ds(index * tok_dev + group * rows, rows)
            rows_ref[span, :] = block[:, group * width : (group + 1) * width]
            mine = lane < 0
            for piece in range(3):
                mine = mine | (lane == me + (group * 3 + piece) * experts)
            weight_ref[span, :] = jnp.broadcast_to(
                jnp.sum(jnp.where(mine, gates, jnp.float32(0.0)), axis=-1, keepdims=True),
                (rows, 128),
            )

    for start in range(0, hidden_width, part):
        columns = pl.ds(start, part)
        tokens = rows_ref[...]
        gate_part = jnp.dot(tokens, gate_ref[0, :, columns], preferred_element_type=jnp.float32)
        up_part = jnp.dot(tokens, up_ref[0, :, columns], preferred_element_type=jnp.float32)
        hidden_ref[:, columns] = (jax.nn.silu(gate_part) * up_part).astype(jnp.bfloat16)

    for start in range(0, width, part):
        columns = pl.ds(start, part)
        output = jnp.dot(
            hidden_ref[...], down_ref[0, :, columns], preferred_element_type=jnp.float32
        )
        output = output * weight_ref[:, :1]
        for index, out in enumerate(outputs):
            out[:, columns] = output[index * tok_dev : (index + 1) * tok_dev].astype(out.dtype)


def run_expert(blocks, kinds, earlier, weights):
    count = len(blocks)
    _, width, hidden = weights[0].shape
    tok_dev = blocks[0].shape[0] * (blocks[0].shape[1] // width)
    rows = count * tok_dev
    inside = [pltpu.with_memory_space_constraint(array, pltpu.VMEM) for array in blocks + weights]
    in_vmem = pl.BlockSpec(memory_space=pltpu.VMEM)
    out_shape = [pltpu.VMEM((tok_dev, width), kind) for kind in kinds]
    return pl.pallas_call(
        functools.partial(expert_kernel, count),
        in_specs=[in_vmem] * len(inside) + [pl.BlockSpec(memory_space=pl.ANY)] * len(earlier),
        out_specs=[in_vmem] * len(out_shape),
        out_shape=out_shape,
        scratch_shapes=[
            pltpu.VMEM((rows, width), jnp.bfloat16),
            pltpu.VMEM((rows, 128), jnp.float32),
            pltpu.VMEM((rows, hidden), jnp.bfloat16),
        ],
        compiler_params=pltpu.CompilerParams(vmem_limit_bytes=16 * 1024 * 1024),
        cost_estimate=pl.CostEstimate(
            flops=6 * rows * width * hidden,
            bytes_accessed=6 * width * hidden + 6 * rows * width,
            transcendentals=rows * hidden,
        ),
    )(*inside, *earlier)


def after(array, others):
    return lax.optimization_barrier([array] + list(others))[0]


def dense_layer(tokens, expert_ids, slot_ids, gate_values, gate_weight, up_weight, down_weight):
    experts = lax.axis_size("ex") * lax.axis_size("ey")
    micro = tokens.shape[0]

    packed = pack(tokens, expert_ids, slot_ids, gate_values)

    long_chains = [(index, 1 if index % 2 == 0 else -1) for index in range(micro)]
    short_chains = [(index, -stride) for index, stride in long_chains]
    chains = [short_chains[1], short_chains[0], long_chains[0], long_chains[1]]
    long_reach, short_reach = experts // 2, (experts - 1) // 2

    gathered = [{0: packed[index]} for index in range(micro)]
    outputs = [{} for index in range(micro)]
    carried = {}

    def gather_hop(some, hop, others):
        for index, stride in some:
            block = gathered[index][-(hop - 1) * stride]
            with jax.named_scope(f"gather{index}_{stride:+d}_hop{hop}"):
                gathered[index][-hop * stride] = pass_on(after(block, others), stride)
            others = others

    def sum_hop(some, left, others):
        sent = []
        for index, stride in some:
            partial = outputs[index][-left * stride]
            before = []
            if (index, stride) in carried:
                before = [carried[index, stride]]
                partial = partial + carried[index, stride].astype(jnp.float32)
            partial = after(partial.astype(jnp.bfloat16), others)
            with jax.named_scope(f"sum{index}_{-stride:+d}_left{left}"):
                carried[index, stride] = pass_on(partial, -stride)
            sent.append(partial)
            others = others
        return sent

    def expert(some, hops, earlier):
        keys = [(index, -hop * stride) for hop in hops for index, stride in some]
        keys = list(dict.fromkeys(keys))
        first = {(index, -long_reach * stride) for index, stride in long_chains}
        first |= {(index, -short_reach * stride) for index, stride in short_chains}
        answers = run_expert(
            [gathered[index][place] for index, place in keys],
            [jnp.bfloat16 if key in first else jnp.float32 for key in keys],
            earlier,
            weights,
        )
        for (index, place), answer in zip(keys, answers):
            outputs[index][place] = answer
        return [answers[0]]

    weights = [gate_weight, up_weight, down_weight]
    marker = mark()
    done = []
    for hop in range(1, short_reach + 1):
        gather_hop(long_chains + short_chains[1:], hop, [marker])
        gather_hop(short_chains[:1], hop, [])
        if hop == short_reach - 1:
            done = expert(chains, range(short_reach - 2, -1, -1), [])
    done = expert(chains, [short_reach - 1], done)
    gather_hop(long_chains, long_reach, done)
    done = expert(long_chains, [short_reach], done)
    done = expert(short_chains[::-1], [short_reach], done)
    last = [gathered[index][-long_reach * stride] for index, stride in long_chains]
    done = expert(long_chains, [long_reach], done)
    for left in range(long_reach, 0, -1):
        sent = sum_hop(long_chains, left, [])
        if left > 1:
            sent = sum_hop(short_chains[:1], left - 1, last + sent)
            sum_hop(short_chains[1:], left - 1, last + sent)

    results = []
    for index in range(micro):
        total = outputs[index][0]
        for stride in (1, -1):
            total = total + carried[index, stride].astype(jnp.float32)
        results.append(total.astype(jnp.bfloat16))
    return jnp.stack(results, axis=0)


def per_device(tokens, expert_ids, slot_ids, gate_values, gate_weight, up_weight, down_weight):
    experts = lax.axis_size("ex") * lax.axis_size("ey")
    layer = dense_layer if experts == expert_ids.shape[-1] else slot_layer
    return layer(
        tokens, expert_ids, slot_ids, gate_values, gate_weight, up_weight, down_weight
    )


def solution(mesh):
    in_specs = (
        P(None, ("dp", "ex", "ey"), None),
        P(None, ("dp", "ex", "ey"), None),
        P(None, ("dp", "ex", "ey"), None),
        P(None, ("dp", "ex", "ey"), None),
        P(("ex", "ey"), None, None),
        P(("ex", "ey"), None, None),
        P(("ex", "ey"), None, None),
    )
    out_specs = P(None, ("dp", "ex", "ey"), None)
    return jax.shard_map(
        per_device, mesh=mesh, in_specs=in_specs, out_specs=out_specs, check_vma=False
    )
```

```python
import functools

import jax
import jax.numpy as jnp
from jax import lax
from jax.experimental import pallas as pl
from jax.experimental.pallas import tpu as pltpu
from jax.sharding import PartitionSpec as P

TOP = 8


def slot_layer(tokens, expert_ids, slot_ids, gate_values, gate_weight, up_weight, down_weight):
    across_x = lax.axis_size("ex")
    across_y = lax.axis_size("ey")
    experts = across_x * across_y
    micro, tok_dev, width = tokens.shape
    slot_count = (tok_dev * TOP * 5 + 4 * experts - 1) // (4 * experts)
    cells = experts * slot_count
    gate_matrix = gate_weight[0]
    up_matrix = up_weight[0]
    down_matrix = down_weight[0]
    columns = jnp.arange(cells, dtype=jnp.int32)

    def expert_apply(received):
        flat = received.reshape(-1, width)
        gate_part = jnp.dot(flat, gate_matrix, preferred_element_type=jnp.float32)
        up_part = jnp.dot(flat, up_matrix, preferred_element_type=jnp.float32)
        hidden = (jax.nn.silu(gate_part) * up_part).astype(jnp.bfloat16)
        output = jnp.dot(hidden, down_matrix, preferred_element_type=jnp.float32).astype(
            jnp.bfloat16
        )
        return output.reshape(received.shape)

    def route_slots(buffer):
        return lax.all_to_all(
            expert_apply(
                lax.all_to_all(buffer, ("ex", "ey"), split_axis=0, concat_axis=0, tiled=True)
            ),
            ("ex", "ey"),
            split_axis=0,
            concat_axis=0,
            tiled=True,
        )

    buffers = []
    mixings = []
    for index in range(micro):
        chosen = expert_ids[index]
        places = slot_ids[index]
        cell_index = jnp.where(places >= 0, chosen * slot_count + places, -1)
        one_hot = cell_index[:, :, None] == columns[None, None, :]
        selection = jnp.sum(one_hot.astype(jnp.float32), axis=1).astype(jnp.bfloat16)
        mixing = jnp.sum(
            jnp.where(one_hot, gate_values[index][:, :, None], jnp.float32(0.0)), axis=1
        )
        gathered = jnp.dot(selection.T, tokens[index], preferred_element_type=jnp.float32)
        buffers.append(gathered.astype(jnp.bfloat16).reshape(experts, slot_count, width))
        mixings.append(mixing)
    outputs = [route_slots(buffers[index]) for index in range(micro)]
    results = []
    for index in range(micro):
        flat_out = outputs[index].reshape(cells, width).astype(jnp.float32)
        mixture = jnp.dot(mixings[index], flat_out, precision=lax.Precision.HIGHEST)
        results.append(mixture.astype(jnp.bfloat16))
    return jnp.stack(results, axis=0)


def pack_kernel(tokens_ref, *refs):
    micro, tok_dev, width = tokens_ref.shape
    routing = refs[:3]
    blocks = refs[3 : 3 + micro]
    ids_ref, slots_ref, gates_ref, spread_ref, small_semaphores, semaphores = refs[3 + micro :]
    choices = ids_ref.shape[1]
    small_copies = [
        pltpu.make_async_copy(source, target, small_semaphores.at[index])
        for index, (source, target) in enumerate(zip(routing, (ids_ref, slots_ref, gates_ref)))
    ]
    rows = blocks[0].shape[0]
    groups = tok_dev // rows
    copies = [
        pltpu.make_async_copy(
            tokens_ref.at[index, pl.ds(group * rows, rows)],
            block.at[:, pl.ds(group * width, width)],
            semaphores.at[index, group],
        )
        for index, block in enumerate(blocks)
        for group in range(groups)
    ]
    for copy in small_copies + copies:
        copy.start()
    for copy in small_copies:
        copy.wait()
    names = lax.broadcasted_iota(jnp.int32, (choices, tok_dev), 0)
    for index, block in enumerate(blocks):
        ids = ids_ref[index]
        kept = jnp.where(slots_ref[index] >= 0, gates_ref[index], jnp.float32(0.0))
        share = jnp.zeros((choices, tok_dev), jnp.float32)
        for choice in range(choices):
            share += jnp.where(
                ids[choice : choice + 1] == names, kept[choice : choice + 1], jnp.float32(0.0)
            )
        spread_ref[...] = jnp.zeros_like(spread_ref)
        for piece in range(3):
            rounded = share.astype(jnp.bfloat16).astype(jnp.float32)
            share = share - rounded
            for group in range(groups):
                place = (group * 3 + piece) * choices
                spread_ref[pl.ds(place, choices), pl.ds(0, rows)] = rounded[
                    :, group * rows : (group + 1) * rows
                ]
        block[:, pl.ds(groups * width, 128)] = spread_ref[...].T[:rows].astype(jnp.bfloat16)
    for copy in copies:
        copy.wait()


def pack(tokens, expert_ids, slot_ids, gate_values):
    micro, tok_dev, width = tokens.shape
    rows = 16
    groups = tok_dev // rows
    columns = [
        jnp.transpose(array, (0, 2, 1)) for array in (expert_ids, slot_ids, gate_values)
    ]
    outside = [
        pltpu.with_memory_space_constraint(array, pltpu.HBM) for array in [tokens] + columns
    ]
    inside = pl.BlockSpec(memory_space=pltpu.VMEM)
    return pl.pallas_call(
        pack_kernel,
        in_specs=[pl.BlockSpec(memory_space=pl.ANY)] * len(outside),
        out_specs=[inside] * micro,
        out_shape=[pltpu.VMEM((rows, groups * width + 128), jnp.bfloat16)] * micro,
        scratch_shapes=[pltpu.VMEM(array.shape, array.dtype) for array in columns]
        + [
            pltpu.VMEM((128, 128), jnp.float32),
            pltpu.SemaphoreType.DMA((len(columns),)),
            pltpu.SemaphoreType.DMA((micro, groups)),
        ],
        compiler_params=pltpu.CompilerParams(vmem_limit_bytes=4 * 1024 * 1024),
        cost_estimate=pl.CostEstimate(
            flops=10_000_000_000, bytes_accessed=0, transcendentals=0
        ),
    )(*outside)


def pass_on(block, stride):
    across_x = lax.axis_size("ex")
    across_y = lax.axis_size("ey")
    ring = []
    for row in range(across_x):
        places = [row * across_y + column for column in range(across_y)]
        ring += places if row % 2 == 0 else places[::-1]
    count = len(ring)
    pairs = [(ring[index], ring[(index + stride) % count]) for index in range(count)]
    return lax.ppermute(block, ("ex", "ey"), pairs)


def expert_kernel(count, *refs):
    blocks = refs[:count]
    gate_ref, up_ref, down_ref = refs[count : count + 3]
    rows_ref, weight_ref, hidden_ref = refs[-3:]
    outputs = refs[-3 - count : -3]
    _, width, hidden_width = gate_ref.shape
    rows = blocks[0].shape[0]
    groups = blocks[0].shape[1] // width
    tok_dev = rows * groups
    part = 256

    me = lax.axis_index("ex") * lax.axis_size("ey") + lax.axis_index("ey")
    experts = lax.axis_size("ex") * lax.axis_size("ey")
    lane = lax.broadcasted_iota(jnp.int32, (rows, 128), 1)
    for index, block in enumerate(blocks):
        gates = block[:, groups * width :].astype(jnp.float32)
        for group in range(groups):
            span = pl.ds(index * tok_dev + group * rows, rows)
            rows_ref[span, :] = block[:, group * width : (group + 1) * width]
            mine = lane < 0
            for piece in range(3):
                mine = mine | (lane == me + (group * 3 + piece) * experts)
            weight_ref[span, :] = jnp.broadcast_to(
                jnp.sum(jnp.where(mine, gates, jnp.float32(0.0)), axis=-1, keepdims=True),
                (rows, 128),
            )

    for start in range(0, hidden_width, part):
        columns = pl.ds(start, part)
        tokens = rows_ref[...]
        gate_part = jnp.dot(tokens, gate_ref[0, :, columns], preferred_element_type=jnp.float32)
        up_part = jnp.dot(tokens, up_ref[0, :, columns], preferred_element_type=jnp.float32)
        hidden_ref[:, columns] = (jax.nn.silu(gate_part) * up_part).astype(jnp.bfloat16)

    for start in range(0, width, part):
        columns = pl.ds(start, part)
        output = jnp.dot(
            hidden_ref[...], down_ref[0, :, columns], preferred_element_type=jnp.float32
        )
        output = output * weight_ref[:, :1]
        for index, out in enumerate(outputs):
            out[:, columns] = output[index * tok_dev : (index + 1) * tok_dev].astype(out.dtype)


def run_expert(blocks, kinds, earlier, weights):
    count = len(blocks)
    _, width, hidden = weights[0].shape
    tok_dev = blocks[0].shape[0] * (blocks[0].shape[1] // width)
    rows = count * tok_dev
    inside = [pltpu.with_memory_space_constraint(array, pltpu.VMEM) for array in blocks + weights]
    in_vmem = pl.BlockSpec(memory_space=pltpu.VMEM)
    out_shape = [pltpu.VMEM((tok_dev, width), kind) for kind in kinds]
    return pl.pallas_call(
        functools.partial(expert_kernel, count),
        in_specs=[in_vmem] * len(inside) + [pl.BlockSpec(memory_space=pl.ANY)] * len(earlier),
        out_specs=[in_vmem] * len(out_shape),
        out_shape=out_shape,
        scratch_shapes=[
            pltpu.VMEM((rows, width), jnp.bfloat16),
            pltpu.VMEM((rows, 128), jnp.float32),
            pltpu.VMEM((rows, hidden), jnp.bfloat16),
        ],
        compiler_params=pltpu.CompilerParams(vmem_limit_bytes=16 * 1024 * 1024),
        cost_estimate=pl.CostEstimate(
            flops=6 * rows * width * hidden,
            bytes_accessed=6 * width * hidden + 6 * rows * width,
            transcendentals=rows * hidden,
        ),
    )(*inside, *earlier)


def after(array, others):
    return lax.optimization_barrier([array] + list(others))[0]


def dense_layer(tokens, expert_ids, slot_ids, gate_values, gate_weight, up_weight, down_weight):
    experts = lax.axis_size("ex") * lax.axis_size("ey")
    micro = tokens.shape[0]

    packed = pack(tokens, expert_ids, slot_ids, gate_values)

    long_chains = [(index, 1 if index % 2 == 0 else -1) for index in range(micro)]
    short_chains = [(index, -stride) for index, stride in long_chains]
    chains = long_chains + short_chains[::-1]
    long_reach, short_reach = experts // 2, (experts - 1) // 2

    gathered = [{0: packed[index]} for index in range(micro)]
    outputs = [{} for index in range(micro)]
    carried = {}

    def gather_hop(some, hop, others):
        for index, stride in some:
            block = gathered[index][-(hop - 1) * stride]
            with jax.named_scope(f"gather{index}_{stride:+d}_hop{hop}"):
                gathered[index][-hop * stride] = pass_on(after(block, others), stride)

    def sum_hop(some, left, others):
        sent = []
        for index, stride in some:
            partial = outputs[index][-left * stride]
            before = []
            if (index, stride) in carried:
                before = [carried[index, stride]]
                partial = partial + carried[index, stride].astype(jnp.float32)
            partial = after(partial.astype(jnp.bfloat16), others)
            with jax.named_scope(f"sum{index}_{-stride:+d}_left{left}"):
                carried[index, stride] = pass_on(partial, -stride)
            sent.append(partial)
        return sent

    def expert(some, hops, earlier):
        keys = [(index, -hop * stride) for hop in hops for index, stride in some]
        keys = list(dict.fromkeys(keys))
        first = {(index, -long_reach * stride) for index, stride in long_chains}
        first |= {(index, -short_reach * stride) for index, stride in short_chains}
        answers = run_expert(
            [gathered[index][place] for index, place in keys],
            [jnp.bfloat16 if key in first else jnp.float32 for key in keys],
            earlier,
            weights,
        )
        for (index, place), answer in zip(keys, answers):
            outputs[index][place] = answer
        return [answers[0]]

    weights = [gate_weight, up_weight, down_weight]
    done = []
    for hop in range(1, short_reach + 1):
        gather_hop(chains, hop, [])
        if hop == 1:
            done = expert(chains, [0], [])
        if hop == short_reach - 1:
            done = expert(chains, range(short_reach - 2, 0, -1), done)
    done = expert(chains, [short_reach - 1], done)
    gather_hop(long_chains, long_reach, done)
    done = expert(chains, [short_reach], done)
    last = [gathered[index][-long_reach * stride] for index, stride in long_chains]
    done = expert(long_chains, [long_reach], done)
    for left in range(long_reach, 0, -1):
        sent = sum_hop(long_chains, left, [])
        if left > 1:
            sent = sum_hop(short_chains[1:], left - 1, last + sent)
            sum_hop(short_chains[:1], left - 1, last + sent)

    results = []
    for index in range(micro):
        total = outputs[index][0]
        for stride in (1, -1):
            total = total + carried[index, stride].astype(jnp.float32)
        results.append(total.astype(jnp.bfloat16))
    return jnp.stack(results, axis=0)


def per_device(tokens, expert_ids, slot_ids, gate_values, gate_weight, up_weight, down_weight):
    experts = lax.axis_size("ex") * lax.axis_size("ey")
    layer = dense_layer if experts == expert_ids.shape[-1] else slot_layer
    return layer(
        tokens, expert_ids, slot_ids, gate_values, gate_weight, up_weight, down_weight
    )


def solution(mesh):
    in_specs = (
        P(None, ("dp", "ex", "ey"), None),
        P(None, ("dp", "ex", "ey"), None),
        P(None, ("dp", "ex", "ey"), None),
        P(None, ("dp", "ex", "ey"), None),
        P(("ex", "ey"), None, None),
        P(("ex", "ey"), None, None),
        P(("ex", "ey"), None, None),
    )
    out_specs = P(None, ("dp", "ex", "ey"), None)
    return jax.shard_map(
        per_device, mesh=mesh, in_specs=in_specs, out_specs=out_specs, check_vma=False
    )
```

```python
import functools

import jax
import jax.numpy as jnp
from jax import lax
from jax.experimental import pallas as pl
from jax.experimental.pallas import tpu as pltpu
from jax.sharding import PartitionSpec as P

TOP = 8


def slot_layer(tokens, expert_ids, slot_ids, gate_values, gate_weight, up_weight, down_weight):
    across_x = lax.axis_size("ex")
    across_y = lax.axis_size("ey")
    experts = across_x * across_y
    micro, tok_dev, width = tokens.shape
    slot_count = (tok_dev * TOP * 5 + 4 * experts - 1) // (4 * experts)
    cells = experts * slot_count
    gate_matrix = gate_weight[0]
    up_matrix = up_weight[0]
    down_matrix = down_weight[0]
    columns = jnp.arange(cells, dtype=jnp.int32)

    def expert_apply(received):
        flat = received.reshape(-1, width)
        gate_part = jnp.dot(flat, gate_matrix, preferred_element_type=jnp.float32)
        up_part = jnp.dot(flat, up_matrix, preferred_element_type=jnp.float32)
        hidden = (jax.nn.silu(gate_part) * up_part).astype(jnp.bfloat16)
        output = jnp.dot(hidden, down_matrix, preferred_element_type=jnp.float32).astype(
            jnp.bfloat16
        )
        return output.reshape(received.shape)

    def route_slots(buffer):
        return lax.all_to_all(
            expert_apply(
                lax.all_to_all(buffer, ("ex", "ey"), split_axis=0, concat_axis=0, tiled=True)
            ),
            ("ex", "ey"),
            split_axis=0,
            concat_axis=0,
            tiled=True,
        )

    buffers = []
    mixings = []
    for index in range(micro):
        chosen = expert_ids[index]
        places = slot_ids[index]
        cell_index = jnp.where(places >= 0, chosen * slot_count + places, -1)
        one_hot = cell_index[:, :, None] == columns[None, None, :]
        selection = jnp.sum(one_hot.astype(jnp.float32), axis=1).astype(jnp.bfloat16)
        mixing = jnp.sum(
            jnp.where(one_hot, gate_values[index][:, :, None], jnp.float32(0.0)), axis=1
        )
        gathered = jnp.dot(selection.T, tokens[index], preferred_element_type=jnp.float32)
        buffers.append(gathered.astype(jnp.bfloat16).reshape(experts, slot_count, width))
        mixings.append(mixing)
    outputs = [route_slots(buffers[index]) for index in range(micro)]
    results = []
    for index in range(micro):
        flat_out = outputs[index].reshape(cells, width).astype(jnp.float32)
        mixture = jnp.dot(mixings[index], flat_out, precision=lax.Precision.HIGHEST)
        results.append(mixture.astype(jnp.bfloat16))
    return jnp.stack(results, axis=0)


def pack_kernel(tokens_ref, *refs):
    micro, tok_dev, width = tokens_ref.shape
    routing = refs[:3]
    blocks = refs[3 : 3 + micro]
    ids_ref, slots_ref, gates_ref, spread_ref, small_semaphores, semaphores = refs[3 + micro :]
    choices = ids_ref.shape[1]
    small_copies = [
        pltpu.make_async_copy(source, target, small_semaphores.at[index])
        for index, (source, target) in enumerate(zip(routing, (ids_ref, slots_ref, gates_ref)))
    ]
    rows = blocks[0].shape[0]
    groups = tok_dev // rows
    copies = [
        pltpu.make_async_copy(
            tokens_ref.at[index, pl.ds(group * rows, rows)],
            block.at[:, pl.ds(group * width, width)],
            semaphores.at[index, group],
        )
        for index, block in enumerate(blocks)
        for group in range(groups)
    ]
    for copy in small_copies + copies:
        copy.start()
    for copy in small_copies:
        copy.wait()
    names = lax.broadcasted_iota(jnp.int32, (choices, tok_dev), 0)
    for index, block in enumerate(blocks):
        ids = ids_ref[index]
        kept = jnp.where(slots_ref[index] >= 0, gates_ref[index], jnp.float32(0.0))
        share = jnp.zeros((choices, tok_dev), jnp.float32)
        for choice in range(choices):
            share += jnp.where(
                ids[choice : choice + 1] == names, kept[choice : choice + 1], jnp.float32(0.0)
            )
        spread_ref[...] = jnp.zeros_like(spread_ref)
        for piece in range(3):
            rounded = share.astype(jnp.bfloat16).astype(jnp.float32)
            share = share - rounded
            for group in range(groups):
                place = (group * 3 + piece) * choices
                spread_ref[pl.ds(place, choices), pl.ds(0, rows)] = rounded[
                    :, group * rows : (group + 1) * rows
                ]
        block[:, pl.ds(groups * width, 128)] = spread_ref[...].T[:rows].astype(jnp.bfloat16)
    for copy in copies:
        copy.wait()


def pack(tokens, expert_ids, slot_ids, gate_values):
    micro, tok_dev, width = tokens.shape
    rows = 16
    groups = tok_dev // rows
    columns = [
        jnp.transpose(array, (0, 2, 1)) for array in (expert_ids, slot_ids, gate_values)
    ]
    outside = [
        pltpu.with_memory_space_constraint(array, pltpu.HBM) for array in [tokens] + columns
    ]
    inside = pl.BlockSpec(memory_space=pltpu.VMEM)
    return pl.pallas_call(
        pack_kernel,
        in_specs=[pl.BlockSpec(memory_space=pl.ANY)] * len(outside),
        out_specs=[inside] * micro,
        out_shape=[pltpu.VMEM((rows, groups * width + 128), jnp.bfloat16)] * micro,
        scratch_shapes=[pltpu.VMEM(array.shape, array.dtype) for array in columns]
        + [
            pltpu.VMEM((128, 128), jnp.float32),
            pltpu.SemaphoreType.DMA((len(columns),)),
            pltpu.SemaphoreType.DMA((micro, groups)),
        ],
        compiler_params=pltpu.CompilerParams(vmem_limit_bytes=4 * 1024 * 1024),
        cost_estimate=pl.CostEstimate(
            flops=10_000_000_000, bytes_accessed=0, transcendentals=0
        ),
    )(*outside)


def pass_on(block, stride):
    across_x = lax.axis_size("ex")
    across_y = lax.axis_size("ey")
    ring = []
    for row in range(across_x):
        places = [row * across_y + column for column in range(across_y)]
        ring += places if row % 2 == 0 else places[::-1]
    count = len(ring)
    pairs = [(ring[index], ring[(index + stride) % count]) for index in range(count)]
    return lax.ppermute(block, ("ex", "ey"), pairs)


def expert_kernel(count, *refs):
    blocks = refs[:count]
    gate_ref, up_ref, down_ref = refs[count : count + 3]
    rows_ref, weight_ref, hidden_ref = refs[-3:]
    outputs = refs[-3 - count : -3]
    _, width, hidden_width = gate_ref.shape
    rows = blocks[0].shape[0]
    groups = blocks[0].shape[1] // width
    tok_dev = rows * groups
    part = 512

    me = lax.axis_index("ex") * lax.axis_size("ey") + lax.axis_index("ey")
    experts = lax.axis_size("ex") * lax.axis_size("ey")
    lane = lax.broadcasted_iota(jnp.int32, (rows, 128), 1)
    for index, block in enumerate(blocks):
        gates = block[:, groups * width :].astype(jnp.float32)
        for group in range(groups):
            span = pl.ds(index * tok_dev + group * rows, rows)
            rows_ref[span, :] = block[:, group * width : (group + 1) * width]
            mine = lane < 0
            for piece in range(3):
                mine = mine | (lane == me + (group * 3 + piece) * experts)
            weight_ref[span, :] = jnp.broadcast_to(
                jnp.sum(jnp.where(mine, gates, jnp.float32(0.0)), axis=-1, keepdims=True),
                (rows, 128),
            )

    for start in range(0, hidden_width, part):
        columns = pl.ds(start, part)
        tokens = rows_ref[...]
        gate_part = jnp.dot(tokens, gate_ref[0, :, columns], preferred_element_type=jnp.float32)
        up_part = jnp.dot(tokens, up_ref[0, :, columns], preferred_element_type=jnp.float32)
        hidden_ref[:, columns] = (jax.nn.silu(gate_part) * up_part).astype(jnp.bfloat16)

    for start in range(0, width, part):
        columns = pl.ds(start, part)
        output = jnp.dot(
            hidden_ref[...], down_ref[0, :, columns], preferred_element_type=jnp.float32
        )
        output = output * weight_ref[:, :1]
        for index, out in enumerate(outputs):
            out[:, columns] = output[index * tok_dev : (index + 1) * tok_dev].astype(out.dtype)


def run_expert(blocks, kinds, earlier, weights):
    count = len(blocks)
    _, width, hidden = weights[0].shape
    tok_dev = blocks[0].shape[0] * (blocks[0].shape[1] // width)
    rows = count * tok_dev
    inside = [pltpu.with_memory_space_constraint(array, pltpu.VMEM) for array in blocks + weights]
    in_vmem = pl.BlockSpec(memory_space=pltpu.VMEM)
    out_shape = [pltpu.VMEM((tok_dev, width), kind) for kind in kinds]
    return pl.pallas_call(
        functools.partial(expert_kernel, count),
        in_specs=[in_vmem] * len(inside) + [pl.BlockSpec(memory_space=pl.ANY)] * len(earlier),
        out_specs=[in_vmem] * len(out_shape),
        out_shape=out_shape,
        scratch_shapes=[
            pltpu.VMEM((rows, width), jnp.bfloat16),
            pltpu.VMEM((rows, 128), jnp.float32),
            pltpu.VMEM((rows, hidden), jnp.bfloat16),
        ],
        compiler_params=pltpu.CompilerParams(vmem_limit_bytes=16 * 1024 * 1024),
        cost_estimate=pl.CostEstimate(
            flops=6 * rows * width * hidden,
            bytes_accessed=6 * width * hidden + 6 * rows * width,
            transcendentals=rows * hidden,
        ),
    )(*inside, *earlier)


def after(array, others):
    return lax.optimization_barrier([array] + list(others))[0]


def dense_layer(tokens, expert_ids, slot_ids, gate_values, gate_weight, up_weight, down_weight):
    experts = lax.axis_size("ex") * lax.axis_size("ey")
    micro = tokens.shape[0]

    packed = pack(tokens, expert_ids, slot_ids, gate_values)

    long_chains = [(index, 1 if index % 2 == 0 else -1) for index in range(micro)]
    short_chains = [(index, -stride) for index, stride in long_chains]
    chains = long_chains + short_chains[::-1]
    long_reach, short_reach = experts // 2, (experts - 1) // 2

    gathered = [{0: packed[index]} for index in range(micro)]
    outputs = [{} for index in range(micro)]
    carried = {}

    def gather_hop(some, hop, others):
        for index, stride in some:
            block = gathered[index][-(hop - 1) * stride]
            with jax.named_scope(f"gather{index}_{stride:+d}_hop{hop}"):
                gathered[index][-hop * stride] = pass_on(after(block, others), stride)

    def sum_hop(some, left, others):
        sent = []
        for index, stride in some:
            partial = outputs[index][-left * stride]
            before = []
            if (index, stride) in carried:
                before = [carried[index, stride]]
                partial = partial + carried[index, stride].astype(jnp.float32)
            partial = after(partial.astype(jnp.bfloat16), others)
            with jax.named_scope(f"sum{index}_{-stride:+d}_left{left}"):
                carried[index, stride] = pass_on(partial, -stride)
            sent.append(partial)
        return sent

    def expert(some, hops, earlier):
        keys = [(index, -hop * stride) for hop in hops for index, stride in some]
        keys = list(dict.fromkeys(keys))
        first = {(index, -long_reach * stride) for index, stride in long_chains}
        first |= {(index, -short_reach * stride) for index, stride in short_chains}
        answers = run_expert(
            [gathered[index][place] for index, place in keys],
            [jnp.bfloat16 if key in first else jnp.float32 for key in keys],
            earlier,
            weights,
        )
        for (index, place), answer in zip(keys, answers):
            outputs[index][place] = answer
        return [answers[0]]

    weights = [gate_weight, up_weight, down_weight]
    done = []
    for hop in range(1, short_reach + 1):
        gather_hop(chains, hop, [])
        if hop == 1:
            done = expert(chains, [0], [])
        if hop == short_reach - 1:
            done = expert(chains, range(short_reach - 2, 0, -1), done)
    done = expert(chains, [short_reach - 1], done)
    gather_hop(long_chains, long_reach, done)
    done = expert(chains, [short_reach], done)
    last = [gathered[index][-long_reach * stride] for index, stride in long_chains]
    done = expert(long_chains, [long_reach], done)
    for left in range(long_reach, 0, -1):
        sent = sum_hop(long_chains, left, [])
        if left > 1:
            sent = sum_hop(short_chains[1:], left - 1, last + sent)
            sum_hop(short_chains[:1], left - 1, last + sent)

    results = []
    for index in range(micro):
        total = outputs[index][0]
        for stride in (1, -1):
            total = total + carried[index, stride].astype(jnp.float32)
        results.append(total.astype(jnp.bfloat16))
    return jnp.stack(results, axis=0)


def per_device(tokens, expert_ids, slot_ids, gate_values, gate_weight, up_weight, down_weight):
    experts = lax.axis_size("ex") * lax.axis_size("ey")
    layer = dense_layer if experts == expert_ids.shape[-1] else slot_layer
    return layer(
        tokens, expert_ids, slot_ids, gate_values, gate_weight, up_weight, down_weight
    )


def solution(mesh):
    in_specs = (
        P(None, ("dp", "ex", "ey"), None),
        P(None, ("dp", "ex", "ey"), None),
        P(None, ("dp", "ex", "ey"), None),
        P(None, ("dp", "ex", "ey"), None),
        P(("ex", "ey"), None, None),
        P(("ex", "ey"), None, None),
        P(("ex", "ey"), None, None),
    )
    out_specs = P(None, ("dp", "ex", "ey"), None)
    return jax.shard_map(
        per_device, mesh=mesh, in_specs=in_specs, out_specs=out_specs, check_vma=False
    )
```

```python
import functools

import jax
import jax.numpy as jnp
from jax import lax
from jax.experimental import pallas as pl
from jax.experimental.pallas import tpu as pltpu
from jax.sharding import PartitionSpec as P

TOP = 8


def slot_layer(tokens, expert_ids, slot_ids, gate_values, gate_weight, up_weight, down_weight):
    across_x = lax.axis_size("ex")
    across_y = lax.axis_size("ey")
    experts = across_x * across_y
    micro, tok_dev, width = tokens.shape
    slot_count = (tok_dev * TOP * 5 + 4 * experts - 1) // (4 * experts)
    cells = experts * slot_count
    gate_matrix = gate_weight[0]
    up_matrix = up_weight[0]
    down_matrix = down_weight[0]
    columns = jnp.arange(cells, dtype=jnp.int32)

    def expert_apply(received):
        flat = received.reshape(-1, width)
        gate_part = jnp.dot(flat, gate_matrix, preferred_element_type=jnp.float32)
        up_part = jnp.dot(flat, up_matrix, preferred_element_type=jnp.float32)
        hidden = (jax.nn.silu(gate_part) * up_part).astype(jnp.bfloat16)
        output = jnp.dot(hidden, down_matrix, preferred_element_type=jnp.float32).astype(
            jnp.bfloat16
        )
        return output.reshape(received.shape)

    def route_slots(buffer):
        return lax.all_to_all(
            expert_apply(
                lax.all_to_all(buffer, ("ex", "ey"), split_axis=0, concat_axis=0, tiled=True)
            ),
            ("ex", "ey"),
            split_axis=0,
            concat_axis=0,
            tiled=True,
        )

    buffers = []
    mixings = []
    for index in range(micro):
        chosen = expert_ids[index]
        places = slot_ids[index]
        cell_index = jnp.where(places >= 0, chosen * slot_count + places, -1)
        one_hot = cell_index[:, :, None] == columns[None, None, :]
        selection = jnp.sum(one_hot.astype(jnp.float32), axis=1).astype(jnp.bfloat16)
        mixing = jnp.sum(
            jnp.where(one_hot, gate_values[index][:, :, None], jnp.float32(0.0)), axis=1
        )
        gathered = jnp.dot(selection.T, tokens[index], preferred_element_type=jnp.float32)
        buffers.append(gathered.astype(jnp.bfloat16).reshape(experts, slot_count, width))
        mixings.append(mixing)
    outputs = [route_slots(buffers[index]) for index in range(micro)]
    results = []
    for index in range(micro):
        flat_out = outputs[index].reshape(cells, width).astype(jnp.float32)
        mixture = jnp.dot(mixings[index], flat_out, precision=lax.Precision.HIGHEST)
        results.append(mixture.astype(jnp.bfloat16))
    return jnp.stack(results, axis=0)


def pack_kernel(tokens_ref, *refs):
    micro, tok_dev, width = tokens_ref.shape
    routing = refs[:3]
    blocks = refs[3 : 3 + micro]
    ids_ref, slots_ref, gates_ref, spread_ref, small_semaphores, semaphores = refs[3 + micro :]
    choices = ids_ref.shape[1]
    small_copies = [
        pltpu.make_async_copy(source, target, small_semaphores.at[index])
        for index, (source, target) in enumerate(zip(routing, (ids_ref, slots_ref, gates_ref)))
    ]
    rows = blocks[0].shape[0]
    groups = tok_dev // rows
    copies = [
        pltpu.make_async_copy(
            tokens_ref.at[index, pl.ds(group * rows, rows)],
            block.at[:, pl.ds(group * width, width)],
            semaphores.at[index, group],
        )
        for index, block in enumerate(blocks)
        for group in range(groups)
    ]
    for copy in small_copies + copies:
        copy.start()
    for copy in small_copies:
        copy.wait()
    names = lax.broadcasted_iota(jnp.int32, (choices, tok_dev), 0)
    for index, block in enumerate(blocks):
        ids = ids_ref[index]
        kept = jnp.where(slots_ref[index] >= 0, gates_ref[index], jnp.float32(0.0))
        share = jnp.zeros((choices, tok_dev), jnp.float32)
        for choice in range(choices):
            share += jnp.where(
                ids[choice : choice + 1] == names, kept[choice : choice + 1], jnp.float32(0.0)
            )
        spread_ref[...] = jnp.zeros_like(spread_ref)
        for piece in range(3):
            rounded = share.astype(jnp.bfloat16).astype(jnp.float32)
            share = share - rounded
            for group in range(groups):
                place = (group * 3 + piece) * choices
                spread_ref[pl.ds(place, choices), pl.ds(0, rows)] = rounded[
                    :, group * rows : (group + 1) * rows
                ]
        block[:, pl.ds(groups * width, 128)] = spread_ref[...].T[:rows].astype(jnp.bfloat16)
    for copy in copies:
        copy.wait()


def pack(tokens, expert_ids, slot_ids, gate_values):
    micro, tok_dev, width = tokens.shape
    rows = 16
    groups = tok_dev // rows
    columns = [
        jnp.transpose(array, (0, 2, 1)) for array in (expert_ids, slot_ids, gate_values)
    ]
    outside = [
        pltpu.with_memory_space_constraint(array, pltpu.HBM) for array in [tokens] + columns
    ]
    inside = pl.BlockSpec(memory_space=pltpu.VMEM)
    return pl.pallas_call(
        pack_kernel,
        in_specs=[pl.BlockSpec(memory_space=pl.ANY)] * len(outside),
        out_specs=[inside] * micro,
        out_shape=[pltpu.VMEM((rows, groups * width + 128), jnp.bfloat16)] * micro,
        scratch_shapes=[pltpu.VMEM(array.shape, array.dtype) for array in columns]
        + [
            pltpu.VMEM((128, 128), jnp.float32),
            pltpu.SemaphoreType.DMA((len(columns),)),
            pltpu.SemaphoreType.DMA((micro, groups)),
        ],
        compiler_params=pltpu.CompilerParams(vmem_limit_bytes=4 * 1024 * 1024),
        cost_estimate=pl.CostEstimate(
            flops=10000000000, bytes_accessed=0, transcendentals=0
        ),
    )(*outside)


def pass_on(block, stride):
    across_x = lax.axis_size("ex")
    across_y = lax.axis_size("ey")
    ring = []
    for row in range(across_x):
        places = [row * across_y + column for column in range(across_y)]
        ring += places if row % 2 == 0 else places[::-1]
    count = len(ring)
    pairs = [(ring[index], ring[(index + stride) % count]) for index in range(count)]
    return lax.ppermute(block, ("ex", "ey"), pairs)


def mark_kernel(marker_ref):
    marker_ref[...] = jnp.zeros_like(marker_ref)


def mark():
    return pl.pallas_call(
        mark_kernel,
        out_specs=pl.BlockSpec(memory_space=pltpu.VMEM),
        out_shape=pltpu.VMEM((8, 128), jnp.float32),
        compiler_params=pltpu.CompilerParams(vmem_limit_bytes=1024 * 1024),
        cost_estimate=pl.CostEstimate(flops=0, bytes_accessed=25000000, transcendentals=0),
    )()


def expert_kernel(count, *refs):
    blocks = refs[:count]
    gate_ref, up_ref, down_ref = refs[count : count + 3]
    rows_ref, weight_ref, hidden_ref = refs[-3:]
    outputs = refs[-3 - count : -3]
    _, width, hidden_width = gate_ref.shape
    rows = blocks[0].shape[0]
    groups = blocks[0].shape[1] // width
    tok_dev = rows * groups
    part = 256

    me = lax.axis_index("ex") * lax.axis_size("ey") + lax.axis_index("ey")
    experts = lax.axis_size("ex") * lax.axis_size("ey")
    lane = lax.broadcasted_iota(jnp.int32, (rows, 128), 1)
    for index, block in enumerate(blocks):
        gates = block[:, groups * width :].astype(jnp.float32)
        for group in range(groups):
            span = pl.ds(index * tok_dev + group * rows, rows)
            rows_ref[span, :] = block[:, group * width : (group + 1) * width]
            mine = lane < 0
            for piece in range(3):
                mine = mine | (lane == me + (group * 3 + piece) * experts)
            weight_ref[span, :] = jnp.broadcast_to(
                jnp.sum(jnp.where(mine, gates, jnp.float32(0.0)), axis=-1, keepdims=True),
                (rows, 128),
            )

    for start in range(0, hidden_width, part):
        columns = pl.ds(start, part)
        tokens = rows_ref[...]
        gate_part = jnp.dot(tokens, gate_ref[0, :, columns], preferred_element_type=jnp.float32)
        up_part = jnp.dot(tokens, up_ref[0, :, columns], preferred_element_type=jnp.float32)
        hidden_ref[:, columns] = (jax.nn.silu(gate_part) * up_part).astype(jnp.bfloat16)

    for start in range(0, width, part):
        columns = pl.ds(start, part)
        output = jnp.dot(
            hidden_ref[...], down_ref[0, :, columns], preferred_element_type=jnp.float32
        )
        output = output * weight_ref[:, :1]
        for index, out in enumerate(outputs):
            out[:, columns] = output[index * tok_dev : (index + 1) * tok_dev].astype(out.dtype)


def run_expert(blocks, kinds, earlier, weights):
    count = len(blocks)
    _, width, hidden = weights[0].shape
    tok_dev = blocks[0].shape[0] * (blocks[0].shape[1] // width)
    rows = count * tok_dev
    inside = [pltpu.with_memory_space_constraint(array, pltpu.VMEM) for array in blocks + weights]
    in_vmem = pl.BlockSpec(memory_space=pltpu.VMEM)
    out_shape = [pltpu.VMEM((tok_dev, width), kind) for kind in kinds]
    return pl.pallas_call(
        functools.partial(expert_kernel, count),
        in_specs=[in_vmem] * len(inside) + [pl.BlockSpec(memory_space=pl.ANY)] * len(earlier),
        out_specs=[in_vmem] * len(out_shape),
        out_shape=out_shape,
        scratch_shapes=[
            pltpu.VMEM((rows, width), jnp.bfloat16),
            pltpu.VMEM((rows, 128), jnp.float32),
            pltpu.VMEM((rows, hidden), jnp.bfloat16),
        ],
        compiler_params=pltpu.CompilerParams(vmem_limit_bytes=16 * 1024 * 1024),
        cost_estimate=pl.CostEstimate(
            flops=6 * rows * width * hidden,
            bytes_accessed=6 * width * hidden + 6 * rows * width,
            transcendentals=rows * hidden,
        ),
    )(*inside, *earlier)


def after(array, others):
    return lax.optimization_barrier([array] + list(others))[0]


def dense_layer(tokens, expert_ids, slot_ids, gate_values, gate_weight, up_weight, down_weight):
    experts = lax.axis_size("ex") * lax.axis_size("ey")
    micro = tokens.shape[0]

    packed = pack(tokens, expert_ids, slot_ids, gate_values)

    long_chains = [(index, 1 if index % 2 == 0 else -1) for index in range(micro)]
    short_chains = [(index, -stride) for index, stride in long_chains]
    chains = [long_chains[0], long_chains[1], short_chains[1], short_chains[0]]
    long_reach, short_reach = experts // 2, (experts - 1) // 2

    gathered = [{0: packed[index]} for index in range(micro)]
    outputs = [{} for index in range(micro)]
    carried = {}

    def gather_hop(some, hop, others):
        for index, stride in some:
            block = gathered[index][-(hop - 1) * stride]
            with jax.named_scope(f"gather{index}_{stride:+d}_hop{hop}"):
                gathered[index][-hop * stride] = pass_on(after(block, others), stride)
            others = others

    def sum_hop(some, left, others):
        sent = []
        for index, stride in some:
            partial = outputs[index][-left * stride]
            before = []
            if (index, stride) in carried:
                before = [carried[index, stride]]
                partial = partial + carried[index, stride].astype(jnp.float32)
            partial = after(partial.astype(jnp.bfloat16), others)
            with jax.named_scope(f"sum{index}_{-stride:+d}_left{left}"):
                carried[index, stride] = pass_on(partial, -stride)
            sent.append(partial)
            others = others
        return sent

    def expert(some, hops, earlier):
        keys = [(index, -hop * stride) for hop in hops for index, stride in some]
        keys = list(dict.fromkeys(keys))
        first = {(index, -long_reach * stride) for index, stride in long_chains}
        first |= {(index, -short_reach * stride) for index, stride in short_chains}
        answers = run_expert(
            [gathered[index][place] for index, place in keys],
            [jnp.bfloat16 if key in first else jnp.float32 for key in keys],
            earlier,
            weights,
        )
        for (index, place), answer in zip(keys, answers):
            outputs[index][place] = answer
        return [answers[0]]

    weights = [gate_weight, up_weight, down_weight]
    marker = mark()
    done = []
    for hop in range(1, short_reach + 1):
        gather_hop(long_chains + short_chains[:1], hop, [marker] + [])
        gather_hop(short_chains[1:], hop, [])
        if hop == 1:
            done = expert(chains, [0], [])
        if hop == short_reach - 1:
            done = expert(chains, range(short_reach - 2, 0, -1), done)
    done = expert(chains, [short_reach - 1], done)
    gather_hop(long_chains, long_reach, done)
    done = expert(long_chains + short_chains[::-1], [short_reach], done)
    last = [gathered[index][-long_reach * stride] for index, stride in long_chains]
    done = expert(long_chains, [long_reach], done)
    for left in range(long_reach, 0, -1):
        sent = sum_hop(long_chains, left, [])
        if left > 1:
            sent = sum_hop(short_chains[:1], left - 1, last + sent)
            sum_hop(short_chains[1:], left - 1, last + sent)

    results = []
    for index in range(micro):
        total = outputs[index][0]
        for stride in (1, -1):
            total = total + carried[index, stride].astype(jnp.float32)
        results.append(total.astype(jnp.bfloat16))
    return jnp.stack(results, axis=0)


def per_device(tokens, expert_ids, slot_ids, gate_values, gate_weight, up_weight, down_weight):
    experts = lax.axis_size("ex") * lax.axis_size("ey")
    layer = dense_layer if experts == expert_ids.shape[-1] else slot_layer
    return layer(
        tokens, expert_ids, slot_ids, gate_values, gate_weight, up_weight, down_weight
    )


def solution(mesh):
    in_specs = (
        P(None, ("dp", "ex", "ey"), None),
        P(None, ("dp", "ex", "ey"), None),
        P(None, ("dp", "ex", "ey"), None),
        P(None, ("dp", "ex", "ey"), None),
        P(("ex", "ey"), None, None),
        P(("ex", "ey"), None, None),
        P(("ex", "ey"), None, None),
    )
    out_specs = P(None, ("dp", "ex", "ey"), None)
    return jax.shard_map(
        per_device, mesh=mesh, in_specs=in_specs, out_specs=out_specs, check_vma=False
    )
```
